512 devices in a mesh: dp: 4 (over x), node: 16 (over z, core), expert: 8 (over y).
Axes of the slice: x: 4, y: 8, z: 8, core: 2. Of those that a mesh axis runs over, the one named last changes fastest.
Arguments:
- x_rollout: bfloat16 [8192, 4096], P(('dp', 'node'), 'expert'), may hold values from -6 to 6
- dest: int32 [8192], P(('dp', 'node')), may hold values from 0 to 8191, as said below
- route_ids: int32 [8192, 4], P(('dp', 'node')), may hold values from 0 to 127, as said below
- route_weights: float32 [8192, 4], P(('dp', 'node')), may hold values from 0.2 to 1
- cotangent: bfloat16 [8192, 4096], P(('dp', 'node'), 'expert'), may hold values from -0.59765625 to 0.59765625
- w_up: bfloat16 [128, 1024, 4096], P(('node', 'expert'), 'dp'), may hold values from -0.09375 to 0.09375
- w_down: bfloat16 [128, 1024, 4096], P(('node', 'expert'), 'dp'), may hold values from -0.1875 to 0.1875
Outputs:
- grad_tokens: bfloat16 [8192, 4096], P(('dp', 'node'), 'expert')
- grad_weights: bfloat16 [8192, 4], P(('dp', 'node'))
The draws below stay inside these ranges and needn't reach their ends.
Inputs may be any that keep to these rules, and one draw needn't show every extreme that they name: `dest`: A permutation of the 8192 rows. Learner shard (d, n) holds rows (d * 16 + n) * 128 to (d * 16 + n) * 128 + 127, and rollout shards are laid out alike. A row of rollout shard (s, n) goes to some learner shard (d, n) of the same n, at a position p within that shard with p mod 4 = s. `route_ids`: each row names 4 different experts, two in each of 2 node groups, listed group by group; expert k lies in node group k // 8. The two groups of a row of learner shard (d, n) are n + o and n + o + 8, modulo 16, for an offset o from 0 to 7 of that row; the two experts of a row in one group lie 4 apart modulo 8. Among the rows of one learner shard at most 24 use any one node group and at most 6 name any one expert; in every shard some node group is used by exactly 24 rows and some expert is named by exactly 6.
All inputs are finite; a program needn't handle non-finite values.
Results may differ from the reference program's by a relative error of at most 0.015.
Values may be sent and summed in bfloat16 or wider, within the bound.
No kernel may reach another device: no remote copies, remote signals or barrier semaphores. Data moves between devices by JAX's collectives and lax.ppermute only.
A program may use at most 64 MiB of HBM per device.

```python
import jax
import jax.numpy as jnp
from jax import lax

D = 4096
H = 1024
GSEL = 2
TOK = 128
EXPERTS = 128
TOP = 4
CAPR = 6
HQ = 256
TOKENS = 8192
N_DP = 4
N_NODE = 16
N_EXPERT = 8


def draw_dest(key, part):
    key = jax.random.fold_in(key, 7)
    share_rows = TOK // N_DP
    blocks = N_DP * N_NODE
    perms = jax.vmap(lambda sub: jax.random.permutation(sub, TOK))(jax.random.split(key, blocks)).astype(jnp.int32)
    block_id = jnp.arange(blocks, dtype=jnp.int32)[:, None]
    source = block_id // N_NODE
    node_id = block_id % N_NODE
    target = perms // share_rows
    within = perms % share_rows
    placed = (target * N_NODE + node_id) * TOK + within * N_DP + source
    return placed.reshape(-1).astype(jnp.int32)


def draw_route_ids(key, part):
    key = jax.random.fold_in(key, 11)
    blocks = N_DP * N_NODE
    group_step = N_NODE // GSEL
    group_cap = 3 * TOK // (2 * group_step)
    half_group = N_EXPERT // 2
    key_rank, key_star, key_shift = jax.random.split(key, 3)
    ranks = jax.vmap(lambda sub: jax.random.permutation(sub, TOK))(jax.random.split(key_rank, blocks)).astype(jnp.int32)
    star = jax.random.randint(key_star, (blocks, 1), 0, group_step).astype(jnp.int32)
    in_star = ranks < group_cap
    others = ranks - group_cap
    offset = jnp.where(in_star, star, (star + 1 + others % (group_step - 1)) % group_step)
    within = jnp.where(in_star, ranks, others // (group_step - 1))
    shift = jax.random.randint(key_shift, (blocks, 1, GSEL), 0, N_EXPERT).astype(jnp.int32)
    node_id = (jnp.arange(blocks, dtype=jnp.int32) % N_NODE)[:, None, None]
    steps_used = jnp.arange(GSEL, dtype=jnp.int32)[None, None, :] * group_step
    groups = (node_id + offset[:, :, None] + steps_used) % N_NODE
    first = (within[:, :, None] + shift) % N_EXPERT
    second = (first + half_group) % N_EXPERT
    chosen = jnp.stack([groups * N_EXPERT + first, groups * N_EXPERT + second], axis=-1)
    return chosen.reshape(blocks * TOK, 2 * GSEL).astype(jnp.int32)


def level_of(rng, shape, pieces, low, largest):
    def one(axis_at, blocks):
        heights = jax.random.uniform(jax.random.fold_in(jax.random.fold_in(rng, 6), axis_at), (blocks,), jnp.float32, low / len(pieces), largest / len(pieces))
        return jnp.repeat(jnp.exp(heights), shape[axis_at] // blocks).reshape((-1,) + (1,) * (len(shape) - axis_at - 1))

    level = one(*pieces[0])
    for cut in pieces[1:]:
        level = level * one(*cut)
    return level


def centred(own_key, shape, spread, bound, shards=(), kind=jnp.bfloat16):
    gain = level_of(own_key, shape, shards, -0.22, 0.18) if shards else 1.0
    values = jax.random.normal(own_key, shape, jnp.float32) * spread * gain
    return jnp.minimum(jnp.maximum(values, -bound), bound).astype(kind)


def setup_inputs(seed: int = 0) -> dict:
    splits = jax.random.split(jax.random.key(seed), 8)
    return {
        "x_rollout": centred(splits[0], (TOKENS, D), 1.0, 6.0, ((0, 64), (1, 8))),
        "dest": draw_dest(jax.random.fold_in(splits[7], 71), 0),
        "route_ids": draw_route_ids(jax.random.fold_in(splits[7], 71), 0),
        "route_weights": jnp.clip(0.2 + 0.8 * jax.random.uniform(splits[3], (TOKENS, TOP), jnp.float32) ** level_of(splits[3], (TOKENS, TOP), ((0, 64),), -0.2, 0.2), 0.2, 1.0),
        "cotangent": centred(splits[4], (TOKENS, D), 0.1, 0.59765625, ((0, 64), (1, 8))),
        "w_up": centred(splits[5], (EXPERTS, H, D), D ** -0.5, 0.09375, ((0, 128), (1, 4))),
        "w_down": centred(splits[6], (EXPERTS, H, D), H ** -0.5, 0.1875, ((0, 128), (1, 4))),
    }


def block_terms(rows_x, rows_dy, up_rows, down_rows):
    pre_act = jnp.dot(rows_x, up_rows.T, preferred_element_type=jnp.float32)
    grad_hidden = jnp.dot(rows_dy, down_rows.T, preferred_element_type=jnp.float32)
    gate_sig = jax.nn.sigmoid(pre_act)
    scores = jnp.sum(pre_act * gate_sig * grad_hidden, axis=1)
    grad_pre = (grad_hidden * gate_sig * (1.0 + pre_act * (1.0 - gate_sig))).astype(jnp.bfloat16)
    partial_value = jnp.dot(grad_pre, up_rows, preferred_element_type=jnp.float32).astype(jnp.bfloat16)
    return partial_value, scores


def reference(x_rollout, dest, route_ids, route_weights, cotangent, w_up, w_down):
    tokens = jnp.zeros_like(x_rollout).at[dest].set(x_rollout)
    token_count, route_count = route_ids.shape
    flat_ids = route_ids.reshape(-1).astype(jnp.int32)
    sort_order = jnp.argsort(flat_ids, stable=True).astype(jnp.int32)
    sorted_ids = flat_ids[sort_order]
    owner_rows = (sort_order // route_count).astype(jnp.int32)
    counts = jnp.bincount(flat_ids, length=EXPERTS).astype(jnp.int32)
    starts = (jnp.cumsum(counts) - counts).astype(jnp.int32)
    capacity = N_DP * N_NODE * CAPR
    padded_rows = jnp.concatenate([owner_rows, jnp.zeros((capacity,), jnp.int32)])

    def one_expert(expert_id):
        index_rows = lax.dynamic_slice_in_dim(padded_rows, starts[expert_id], capacity)
        live = jnp.arange(capacity, dtype=jnp.int32) < counts[expert_id]
        rows_x = jnp.where(live[:, None], tokens[index_rows], jnp.zeros((), tokens.dtype))
        rows_dy = jnp.where(live[:, None], cotangent[index_rows], jnp.zeros((), cotangent.dtype))
        up_all = w_up[expert_id]
        down_all = w_down[expert_id]
        summed = jnp.zeros((capacity, D), jnp.float32)
        scores = jnp.zeros((capacity,), jnp.float32)
        for block in range(N_DP):
            partial_value, part_scores = block_terms(rows_x, rows_dy, up_all[block * HQ:(block + 1) * HQ],
                                               down_all[block * HQ:(block + 1) * HQ])
            summed = summed + lax.optimization_barrier(partial_value).astype(jnp.float32)
            scores = scores + part_scores
        return summed.astype(jnp.bfloat16), scores.astype(jnp.bfloat16)

    expert_rows, expert_scores = lax.map(one_expert, jnp.arange(EXPERTS, dtype=jnp.int32))
    offsets = jnp.arange(flat_ids.shape[0], dtype=jnp.int32) - starts[sorted_ids]
    rows_sorted = expert_rows[sorted_ids, offsets]
    scores_sorted = expert_scores[sorted_ids, offsets]
    route_rows = jnp.zeros_like(rows_sorted).at[sort_order].set(rows_sorted).reshape(token_count, route_count, -1)
    route_scores = jnp.zeros_like(scores_sorted).at[sort_order].set(scores_sorted).reshape(token_count, route_count)
    grad_tokens = jnp.sum(route_weights[:, :, None] * route_rows.astype(jnp.float32), axis=1).astype(jnp.bfloat16)
    return grad_tokens, route_scores
```

```python
import functools

import jax
import jax.numpy as jnp
import numpy as np
from jax import lax
from jax.experimental import pallas as pl
from jax.experimental.pallas import tpu as pltpu
from jax.sharding import PartitionSpec as P

BF = jnp.bfloat16
F32 = jnp.float32
CAP = 6
TOK = 128
WID = 512
LANE = 128
PARAMS = pltpu.CompilerParams(vmem_limit_bytes=32 * 1024 * 1024)


def np_pack():
    m = np.zeros((384, 384), np.float32)
    for k in range(8):
        for a in range(8):
            for s in range(6):
                m[k * 48 + a * 6 + s, a * 48 + s * 8 + k] = 1
    return m


def np_unpack():
    m = np.zeros((384, 384), np.float32)
    for n in range(8):
        for a in range(8):
            for s in range(6):
                m[a * 48 + n * 6 + s, n * 48 + a * 6 + s] = 1
    return m


def np_reply():
    m = np.zeros((256, 256), np.float32)
    for n in range(8):
        for s in range(6):
            for c in range(4):
                m[n * 32 + c * 6 + s, c * 48 + n * 6 + s] = 1
            m[n * 32 + 24, 192 + n * 6 + s] = 1
    return m


def np_collect():
    m = np.zeros((208, 256), np.float32)
    for k in range(8):
        for c in range(4):
            for s in range(6):
                m[c * 48 + k * 6 + s, k * 32 + c * 6 + s] = 1
        m[192 + k, k * 32 + 24] = 1
    return m


def np_slot_mask():
    m = np.zeros((96, LANE), np.float32)
    for r in range(96):
        m[r, r % 6] = 1
    return m


def iota(shape, dim):
    return lax.broadcasted_iota(jnp.int32, shape, dim)


def dot(a, b):
    return jnp.dot(a, b, preferred_element_type=F32)


def dot_nt(a, b):
    return lax.dot_general(a, b, (((1,), (1,)), ((), ())), preferred_element_type=F32)


def dot_tn(a, b):
    return lax.dot_general(a, b, (((0,), (0,)), ((), ())), preferred_element_type=F32)


def named_by(info):
    experts = iota((TOK, LANE), 1).astype(F32)
    named = jnp.zeros((TOK, LANE), F32)
    for j in range(4):
        named = named + jnp.where(info[:, j:j + 1] == experts, 1.0, 0.0)
    return named


def prepare_kernel(shard_step, x_ref, dest_ref, dy_ref, ids_ref, w_ref, sorted_ref, pay_ref):
    dest = dest_ref[...]
    target = (dest // shard_step) * 32 + (dest % TOK) // 4
    pick = jnp.where(iota((TOK, TOK), 0) == target, 1.0, 0.0).astype(BF)
    sorted_ref[...] = dot(pick, x_ref[...]).astype(BF)
    pay_ref[:, :WID] = dy_ref[...]
    lanes = iota((TOK, LANE), 1)
    info = jnp.zeros((TOK, LANE), F32)
    ids = ids_ref[...].astype(F32)
    weights = w_ref[...]
    for j in range(4):
        info = jnp.where(lanes == j, ids[:, j:j + 1], info)
        rest = weights[:, j:j + 1]
        for piece in range(3):
            part = rest.astype(BF).astype(F32)
            info = jnp.where(lanes == 4 + 4 * piece + j, part, info)
            rest = rest - part
    pay_ref[:, WID:] = info.astype(BF)


def pack_kernel(pay_ref, x_ref, perm_ref, out_ref, slots, rows):
    info = pay_ref[:, WID:].astype(F32)
    named = named_by(info).astype(BF)
    earlier = jnp.where(iota((TOK, TOK), 0) < iota((TOK, TOK), 1), 1.0, 0.0).astype(BF)
    same = jnp.where(iota((TOK, TOK), 0) == iota((TOK, TOK), 1), 1.0, 0.0).astype(BF)
    rank = dot_tn(named, earlier)
    named_t = dot_tn(named, same)
    for s in range(CAP):
        slots[s] = jnp.where(rank == float(s), named_t, 0.0)
    token = iota((TOK, TOK), 0)
    order = jnp.where(iota((TOK, TOK), 1) == (token % 4) * 32 + token // 4, 1.0, 0.0).astype(BF)
    rows[:, :WID] = pay_ref[:, :WID]
    rows[:, WID:] = dot(order, x_ref[...]).astype(BF)
    perm = perm_ref[...]
    for pair in range(8):
        halves = []
        for block in (2 * pair, 2 * pair + 1):
            pick = jnp.concatenate([slots[s, block * 8:block * 8 + 8, :] for s in range(CAP)], axis=0).astype(BF)
            got = dot(pick, rows[...]).astype(BF)
            halves.append(jnp.concatenate([got[:, a * LANE:(a + 1) * LANE] for a in range(8)], axis=0))
        sent = dot(perm, jnp.concatenate(halves, axis=1)).astype(BF)
        for h in range(2):
            out_ref[(2 * pair + h) * 8:(2 * pair + h) * 8 + 8] = sent[:, h * LANE:(h + 1) * LANE].reshape(8, 48, LANE)


def forward_kernel(me_ref, got_ref, w0, w1, w2, w3, perm_ref, out_ref, dy_rows, x_rows):
    perm = perm_ref[...]
    for d in range(4):
        for half in range(2):
            base = d * 96 + half * 48
            both = jnp.concatenate(
                [got_ref[half * 8:half * 8 + 8, 2 * d + b].reshape(384, LANE) for b in range(2)], axis=1
            )
            moved = dot(perm, both).astype(BF)
            for a in range(8):
                target = dy_rows if a < 4 else x_rows
                for b in range(2):
                    col = (b * 4 + a % 4) * LANE
                    target[base:base + 48, col:col + LANE] = moved[a * 48:a * 48 + 48, b * LANE:(b + 1) * LANE]
    me = me_ref[0]
    for k, w in enumerate((w0, w1, w2, w3)):
        block = lax.rem(me - k + 4, 4)
        pre = dot_nt(x_rows[...], w[:256]).astype(BF)
        grad = dot_nt(dy_rows[...], w[256:]).astype(BF)
        out_ref[:, block, :, :256] = pre.reshape(4, 96, 256)
        out_ref[:, block, :, 256:] = grad.reshape(4, 96, 256)


def act_kernel(part_ref, mask_ref, out_ref):
    score = jnp.zeros((96, 1), F32)
    for block in range(4):
        total = part_ref[0, block].astype(F32)
        for s in range(1, 4):
            total = total + part_ref[s, block].astype(F32)
        pre = total[:, :256]
        grad = total[:, 256:]
        sig = jax.nn.sigmoid(pre)
        score = score + jnp.sum(pre * sig * grad, axis=1, keepdims=True)
        out_ref[:, block * 256:block * 256 + 256] = (grad * sig * (1.0 + pre * (1.0 - sig))).astype(BF)
    out_ref[:, 1024:] = (score * mask_ref[...].astype(F32)).astype(BF)


def backward_kernel(me_ref, grad_ref, w0, w1, w2, w3, perm_ref, out_ref, rows):
    me = me_ref[0]
    total = jnp.zeros((384, 1024), F32)
    for k, w in enumerate((w0, w1, w2, w3)):
        block = lax.rem(me - k + 4, 4)
        part = grad_ref[:, :, pl.ds(pl.multiple_of(block * 256, 256), 256)].reshape(384, 256)
        total = total + dot(part, w[...])
    rows[...] = total.astype(BF)
    perm = perm_ref[...]
    for d in range(4):
        for half in range(2):
            base = d * 96 + half * 48
            score = grad_ref[d, half * 48:half * 48 + 48, 1024:]
            stacks = []
            for b in range(2):
                parts = [rows[base:base + 48, (b * 4 + c) * LANE:(b * 4 + c + 1) * LANE] for c in range(4)]
                stacks.append(jnp.concatenate(parts + [score, jnp.zeros((16, LANE), BF)], axis=0))
            sent = dot(perm, jnp.concatenate(stacks, axis=1)).astype(BF)
            for b in range(2):
                out_ref[half * 8:half * 8 + 8, 2 * d + b] = sent[:, b * LANE:(b + 1) * LANE].reshape(8, 32, LANE)


def combine_kernel(got_ref, info_ref, perm_ref, out_ref, rows, scores):
    info = info_ref[...].astype(F32)
    named = named_by(info).astype(BF)
    later = jnp.where(iota((TOK, TOK), 1) < iota((TOK, TOK), 0), 1.0, 0.0).astype(BF)
    rank = dot(later, named)
    perm = perm_ref[...]
    for pair in range(8):
        both = jnp.concatenate(
            [got_ref[(2 * pair + h) * 8:(2 * pair + h) * 8 + 8].reshape(256, LANE) for h in range(2)], axis=1
        )
        moved = dot(perm, both)
        for h in range(2):
            block = 2 * pair + h
            half = moved[:, h * LANE:(h + 1) * LANE]
            scores[block * 8:block * 8 + 8] = half[192:200]
            for c in range(4):
                rows[block * 48:block * 48 + 48, c * LANE:(c + 1) * LANE] = half[c * 48:c * 48 + 48].astype(BF)
    lanes = iota((TOK, LANE), 1).astype(F32)
    wide = iota((TOK, 128 * CAP), 1).astype(F32)
    coefs = [jnp.zeros((TOK, 128 * CAP), F32) for _ in range(3)]
    table = scores[...].astype(BF)
    back = jnp.zeros((TOK, LANE), F32)
    for j in range(4):
        expert = info[:, j:j + 1]
        mine = expert == lanes
        slot = jnp.sum(jnp.where(mine, rank, 0.0), axis=1, keepdims=True)
        here = wide == expert * float(CAP) + slot
        for p in range(3):
            coefs[p] = jnp.where(here, info[:, 4 + 4 * p + j:5 + 4 * p + j], coefs[p])
        line = dot(jnp.where(mine, 1.0, 0.0).astype(BF), table)
        value = jnp.sum(jnp.where(lanes == slot, line, 0.0), axis=1, keepdims=True)
        back = jnp.where(lanes == float(j), value, back)
    values = rows[...]
    total = dot(coefs[0].astype(BF), values) + (dot(coefs[1].astype(BF), values) + dot(coefs[2].astype(BF), values))
    out_ref[:, :WID] = total.astype(BF)
    out_ref[:, WID:] = back.astype(BF)


VM = pl.BlockSpec(memory_space=pltpu.VMEM)
SM = pl.BlockSpec(memory_space=pltpu.SMEM)


def call(kernel, out_shape, args, in_specs=None, scratch=(), name=None):
    return pl.pallas_call(
        kernel,
        out_shape=out_shape,
        in_specs=in_specs or [VM] * len(args),
        out_specs=jax.tree.map(lambda _: VM, out_shape),
        scratch_shapes=list(scratch),
        compiler_params=PARAMS,
        name=name,
    )(*args)


def struct(shape):
    return jax.ShapeDtypeStruct(shape, BF)


def shards(x_rollout, dest, route_ids, route_weights, cotangent, w_up, w_down):
    dp = lax.axis_size("dp")
    node = lax.axis_size("node")
    group = lax.axis_size("expert")
    me = lax.axis_index("dp")
    me_arr = me.reshape(1).astype(jnp.int32)
    swap = [(d * group + e, (e // 2) * group + 2 * d + e % 2) for d in range(dp) for e in range(group)]
    plane = ("node", "expert")

    sorted_x, pay = call(
        functools.partial(prepare_kernel, node * TOK),
        (struct((TOK, WID)), struct((TOK, WID + LANE))),
        (x_rollout, dest.reshape(1, TOK), cotangent, route_ids, route_weights),
        name="prepare",
    )
    pay = lax.ppermute(pay, ("dp", "expert"), swap)
    arrived = lax.all_to_all(sorted_x.reshape(dp, 32, WID), "dp", split_axis=0, concat_axis=0, tiled=True)
    moved_x = lax.ppermute(arrived.reshape(TOK, WID), ("dp", "expert"), swap)

    up, down = w_up[0], w_down[0]
    blocks = []
    for k in range(dp):
        start = lax.rem(me + k, dp) * 1024
        block = jnp.concatenate(
            [lax.dynamic_slice_in_dim(up, start, 1024, 1), lax.dynamic_slice_in_dim(down, start, 1024, 1)], axis=0
        )
        blocks.append(lax.ppermute(block, "dp", [(i, (i + k) % dp) for i in range(dp)]) if k else block)

    send = call(
        pack_kernel,
        struct((128, 48, LANE)),
        (pay, moved_x, jnp.asarray(np_pack(), BF)),
        scratch=(pltpu.VMEM((CAP, TOK, LANE), F32), pltpu.VMEM((TOK, 2 * WID), BF)),
        name="pack",
    )
    got = lax.all_to_all(send, plane, split_axis=0, concat_axis=0, tiled=True)
    part = call(
        forward_kernel,
        struct((4, 4, 96, WID)),
        (me_arr, got.reshape(node, group, 48, LANE), *blocks, jnp.asarray(np_unpack(), BF)),
        in_specs=[SM] + [VM] * 6,
        scratch=(pltpu.VMEM((384, 1024), BF), pltpu.VMEM((384, 1024), BF)),
        name="forward",
    )
    part = lax.all_to_all(part, "dp", split_axis=0, concat_axis=0, tiled=True)
    grad = call(act_kernel, struct((96, 1024 + LANE)), (part, jnp.asarray(np_slot_mask(), BF)), name="act")
    grads = lax.all_gather(grad, "dp", axis=0, tiled=False)
    reply = pl.pallas_call(
        backward_kernel,
        grid=(1,),
        out_shape=struct((node, group, 32, LANE)),
        in_specs=[SM, VM] + [pl.BlockSpec((256, 1024), lambda i: (0, 0))] * 4 + [VM],
        out_specs=VM,
        scratch_shapes=[pltpu.VMEM((384, 1024), BF)],
        compiler_params=PARAMS,
        name="backward",
    )(me_arr, grads, *blocks, jnp.asarray(np_reply(), BF))
    back = lax.all_to_all(reply.reshape(128, 32, LANE), plane, split_axis=0, concat_axis=0, tiled=True)
    result = call(
        combine_kernel,
        struct((TOK, WID + LANE)),
        (back, pay[:, WID:], jnp.asarray(np_collect(), BF)),
        scratch=(pltpu.VMEM((128 * CAP, WID), BF), pltpu.VMEM((LANE, LANE), F32)),
        name="combine",
    )
    result = lax.ppermute(result, ("dp", "expert"), swap)
    return result[:, :WID], result[:, WID:WID + 4]


def solution(mesh):
    in_specs = (
        P(("dp", "node"), "expert"),
        P(("dp", "node")),
        P(("dp", "node"), None),
        P(("dp", "node"), None),
        P(("dp", "node"), "expert"),
        P(("node", "expert"), "dp", None),
        P(("node", "expert"), "dp", None),
    )
    out_specs = (P(("dp", "node"), "expert"), P(("dp", "node"), None))
    return jax.shard_map(shards, mesh=mesh, in_specs=in_specs, out_specs=out_specs, check_vma=False)
```

```python
import functools

import jax
import jax.numpy as jnp
from jax import lax
from jax.experimental import pallas as pl
from jax.experimental.pallas import tpu as pltpu
from jax.sharding import PartitionSpec as P

BF = jnp.bfloat16
F32 = jnp.float32
CAP = 6
TOK = 128
WID = 512
INFO = 16
LANE = 128
GATHER_BYTES = 200_000_000
PARAMS = pltpu.CompilerParams(vmem_limit_bytes=20 * 1024 * 1024)


def iota(shape, dim):
    return lax.broadcasted_iota(jnp.int32, shape, dim)


def split(index, base):
    high = jnp.floor((index + 0.5) * (1.0 / base))
    return high, index - high * base


def order_matrix(rows, columns, source):
    row = iota((rows, 1), 0).astype(F32)
    return jnp.where(iota((rows, columns), 1).astype(F32) == source(row), 1.0, 0.0).astype(BF)


def pack_source(row):
    expert, rest = split(row, 48)
    chunk, slot = split(rest, CAP)
    return chunk * 48 + slot * 8 + expert


def unpack_source(row):
    chunk, rest = split(row, 48)
    node, slot = split(rest, CAP)
    return node * 48 + chunk * CAP + slot


def collect_source(row):
    chunk, rest = split(row, 48)
    expert, slot = split(rest, CAP)
    return jnp.where(row < 192, expert * 32 + chunk * CAP + slot, jnp.where(row < 200, (row - 192) * 32 + 24, -1.0))


def reply_matrix():
    column = iota((1, 256), 1).astype(F32)
    chunk, rest = split(column, 48)
    node, slot = split(rest, CAP)
    target = jnp.where(column < 192, node * 32 + chunk * CAP + slot, jnp.where(column < 240, node * 32 + 24, -1.0))
    return jnp.where(iota((256, 256), 0).astype(F32) == target, 1.0, 0.0).astype(BF)


def dot(a, b):
    return jnp.dot(a, b, preferred_element_type=F32)


def dot_nt(a, b):
    return lax.dot_general(a, b, (((1,), (1,)), ((), ())), preferred_element_type=F32)


def dot_tn(a, b):
    return lax.dot_general(a, b, (((0,), (0,)), ((), ())), preferred_element_type=F32)


def named_rows(info):
    experts = iota((LANE, TOK), 0).astype(F32)
    named = jnp.zeros((LANE, TOK), F32)
    for j in range(4):
        named = named + jnp.where(info[j:j + 1, :] == experts, 1.0, 0.0)
    earlier = jnp.where(iota((TOK, TOK), 0) < iota((TOK, TOK), 1), 1.0, 0.0).astype(BF)
    return named, dot(named.astype(BF), earlier)


def prepare_kernel(shard_step, x_any, dest_any, dy_any, ids_any, w_any, sorted_ref, pay_ref,
                   x_ref, dest_ref, ids_ref, w_ref, sems):
    copies = [
        pltpu.make_async_copy(source, target, sems.at[i])
        for i, (source, target) in enumerate((
            (dest_any, dest_ref), (ids_any, ids_ref), (w_any, w_ref), (x_any, x_ref), (dy_any, pay_ref.at[:TOK]),
        ))
    ]
    for copy in copies:
        copy.start()
    pay_ref[TOK:, LANE:] = jnp.zeros((INFO, WID - LANE), BF)
    for copy in copies:
        copy.wait()
    dest = dest_ref[...]
    target = (dest // shard_step) * 32 + (dest % TOK) // 4
    pick = jnp.where(iota((TOK, TOK), 0) == target, 1.0, 0.0).astype(BF)
    sorted_ref[...] = dot(pick, x_ref[...]).astype(BF)
    weights = w_ref[...]
    high = weights.astype(BF).astype(F32)
    middle = (weights - high).astype(BF).astype(F32)
    low = weights - high - middle
    pay_ref[TOK:, :LANE] = jnp.concatenate([ids_ref[...].astype(F32), high, middle, low], axis=0).astype(BF)


def split_kernel(me_ref, up_ref, down_ref, after_ref, *refs):
    outs, sems = refs[:4], refs[4]
    copies = []
    for k in range(4):
        start = pl.multiple_of(lax.rem(me_ref[0] + k, 4) * 1024, 1024)
        for h, w in enumerate((up_ref, down_ref)):
            copies.append(pltpu.make_async_copy(
                w.at[:, pl.ds(start, 1024)], outs[k].at[h * 256:h * 256 + 256], sems.at[2 * k + h]
            ))
    for copy in copies:
        copy.start()
    for copy in copies:
        copy.wait()


def pack_kernel(pay_ref, x_ref, out_ref, slots, rows):
    named, rank = named_rows(pay_ref[TOK:, :LANE].astype(F32))
    for s in range(CAP):
        slots[s] = jnp.where(rank == float(s), named, 0.0)
    token = iota((TOK, TOK), 0)
    order = jnp.where(iota((TOK, TOK), 1) == (token % 4) * 32 + token // 4, 1.0, 0.0).astype(BF)
    rows[:, :WID] = pay_ref[:TOK, :]
    rows[:, WID:] = dot(order, x_ref[...]).astype(BF)
    perm = order_matrix(384, 384, pack_source)
    for pair in range(8):
        halves = []
        for block in (2 * pair, 2 * pair + 1):
            pick = jnp.concatenate([slots[s, block * 8:block * 8 + 8, :] for s in range(CAP)], axis=0).astype(BF)
            got = dot(pick, rows[...]).astype(BF)
            halves.append(jnp.concatenate([got[:, a * LANE:(a + 1) * LANE] for a in range(8)], axis=0))
        sent = dot(perm, jnp.concatenate(halves, axis=1)).astype(BF)
        for h in range(2):
            out_ref[(2 * pair + h) * 8:(2 * pair + h) * 8 + 8] = sent[:, h * LANE:(h + 1) * LANE].reshape(8, 48, LANE)


def gather_kernel(me_ref, w0, w1, w2, w3, out_ref):
    me = me_ref[0]
    for k, w in enumerate((w0, w1, w2, w3)):
        block = lax.rem(me - k + 4, 4)
        out_ref[0, block] = w[:256]
        out_ref[1, block] = w[256:]


def forward_kernel(me_ref, got_ref, w_ref, out_ref, dy_rows, x_rows):
    perm = order_matrix(384, 384, unpack_source)
    me = me_ref[0]
    for d in range(4):
        place = 2 * jnp.bitwise_xor(me, d)
        for half in range(2):
            base = d * 96 + half * 48
            both = jnp.concatenate(
                [got_ref[half * 8:half * 8 + 8, place + b].reshape(384, LANE) for b in range(2)], axis=1
            )
            moved = dot(perm, both).astype(BF)
            for a in range(8):
                target = dy_rows if a < 4 else x_rows
                for b in range(2):
                    col = (b * 4 + a % 4) * LANE
                    target[base:base + 48, col:col + LANE] = moved[a * 48:a * 48 + 48, b * LANE:(b + 1) * LANE]
    for block in range(4):
        pre = dot_nt(x_rows[...], w_ref[0, block]).astype(BF)
        grad = dot_nt(dy_rows[...], w_ref[1, block]).astype(BF)
        out_ref[:, block, :, :256] = pre.reshape(4, 96, 256)
        out_ref[:, block, :, 256:] = grad.reshape(4, 96, 256)


def act_kernel(part_ref, out_ref):
    score = jnp.zeros((96, 1), F32)
    for block in range(4):
        total = part_ref[0, block].astype(F32)
        for s in range(1, 4):
            total = total + part_ref[s, block].astype(F32)
        pre = total[:, :256]
        grad = total[:, 256:]
        sig = jax.nn.sigmoid(pre)
        score = score + jnp.sum(pre * sig * grad, axis=1, keepdims=True)
        out_ref[:, block * 256:block * 256 + 256] = (grad * sig * (1.0 + pre * (1.0 - sig))).astype(BF)
    _, slot = split(iota((96, 1), 0).astype(F32), CAP)
    out_ref[:, 1024:] = jnp.where(iota((96, LANE), 1).astype(F32) == slot, score, 0.0).astype(BF)


def backward_kernel(me_ref, grad_ref, w_ref, out_ref, rows):
    total = jnp.zeros((384, 1024), F32)
    for block in range(4):
        part = grad_ref[:, :, block * 256:block * 256 + 256].reshape(384, 256)
        total = total + dot(part, w_ref[0, block])
    rows[...] = total.astype(BF)
    perm = reply_matrix()
    me = me_ref[0]
    for d in range(4):
        place = 2 * jnp.bitwise_xor(me, d)
        for half in range(2):
            base = d * 96 + half * 48
            score = grad_ref[d, half * 48:half * 48 + 48, 1024:]
            stacks = []
            for b in range(2):
                parts = [rows[base:base + 48, (b * 4 + c) * LANE:(b * 4 + c + 1) * LANE] for c in range(4)]
                stacks.append(jnp.concatenate(parts + [score, jnp.zeros((16, LANE), BF)], axis=0))
            sent = dot(perm, jnp.concatenate(stacks, axis=1)).astype(BF)
            for b in range(2):
                out_ref[half * 8:half * 8 + 8, place + b] = sent[:, b * LANE:(b + 1) * LANE].reshape(8, 32, LANE)


def combine_kernel(got_ref, pay_ref, out_ref, rows, scores):
    info_rows = pay_ref[TOK:, :LANE]
    named, rank_rows = named_rows(info_rows.astype(F32))
    eye = jnp.where(iota((TOK, TOK), 0) == iota((TOK, TOK), 1), 1.0, 0.0).astype(BF)
    rank = dot_tn(rank_rows.astype(BF), eye)
    info = dot_tn(info_rows, eye[:INFO])
    perm = order_matrix(208, 256, collect_source)
    for pair in range(8):
        both = jnp.concatenate(
            [got_ref[(2 * pair + h) * 8:(2 * pair + h) * 8 + 8].reshape(256, LANE) for h in range(2)], axis=1
        )
        moved = dot(perm, both)
        for h in range(2):
            block = 2 * pair + h
            half = moved[:, h * LANE:(h + 1) * LANE]
            scores[block * 8:block * 8 + 8] = half[192:200]
            for c in range(4):
                rows[block * 48:block * 48 + 48, c * LANE:(c + 1) * LANE] = half[c * 48:c * 48 + 48].astype(BF)
    lanes = iota((TOK, LANE), 1).astype(F32)
    wide = iota((TOK, 128 * CAP), 1).astype(F32)
    coefs = [jnp.zeros((TOK, 128 * CAP), F32) for _ in range(3)]
    table = scores[...].astype(BF)
    back = jnp.zeros((TOK, LANE), F32)
    for j in range(4):
        expert = info[:, j:j + 1]
        mine = expert == lanes
        slot = jnp.sum(jnp.where(mine, rank, 0.0), axis=1, keepdims=True)
        here = wide == expert * float(CAP) + slot
        for p in range(3):
            coefs[p] = jnp.where(here, info[:, 4 + 4 * p + j:5 + 4 * p + j], coefs[p])
        line = dot(jnp.where(mine, 1.0, 0.0).astype(BF), table)
        value = jnp.sum(jnp.where(lanes == slot, line, 0.0), axis=1, keepdims=True)
        back = jnp.where(lanes == float(j), value, back)
    values = rows[...]
    total = dot(coefs[0].astype(BF), values) + (dot(coefs[1].astype(BF), values) + dot(coefs[2].astype(BF), values))
    out_ref[:TOK, :] = total.astype(BF)
    out_ref[TOK:, :LANE] = dot_tn(back.astype(BF), eye)[:INFO].astype(BF)
    out_ref[TOK:, LANE:] = jnp.zeros((INFO, WID - LANE), BF)


VM = pl.BlockSpec(memory_space=pltpu.VMEM)
SM = pl.BlockSpec(memory_space=pltpu.SMEM)
HBM = pl.BlockSpec(memory_space=pltpu.HBM)


def call(kernel, out_shape, args, in_specs=None, scratch=(), name=None, cost=None, out_spec=VM, params=PARAMS):
    return pl.pallas_call(
        kernel,
        out_shape=out_shape,
        in_specs=in_specs or [VM] * len(args),
        out_specs=jax.tree.map(lambda _: out_spec, out_shape),
        scratch_shapes=list(scratch),
        compiler_params=params,
        cost_estimate=cost,
        name=name,
    )(*args)


def struct(shape):
    return jax.ShapeDtypeStruct(shape, BF)


def shards(x_rollout, dest, route_ids, route_weights, cotangent, w_up, w_down):
    dp = lax.axis_size("dp")
    node = lax.axis_size("node")
    group = lax.axis_size("expert")
    me = lax.axis_index("dp")
    me_arr = me.reshape(1).astype(jnp.int32)
    swap = [(d * group + e, (e // 2) * group + 2 * (d ^ (e // 2)) + e % 2) for d in range(dp) for e in range(group)]
    swap_back = [(to, source) for source, to in swap]
    plane = ("node", "expert")

    sorted_x, pay = call(
        functools.partial(prepare_kernel, node * TOK),
        (struct((TOK, WID)), struct((TOK + INFO, WID))),
        (x_rollout, dest.reshape(1, TOK), cotangent, route_ids.T, route_weights.T),
        in_specs=[HBM] * 5,
        scratch=(
            pltpu.VMEM((TOK, WID), BF), pltpu.VMEM((1, TOK), jnp.int32), pltpu.VMEM((4, TOK), jnp.int32),
            pltpu.VMEM((4, TOK), F32), pltpu.SemaphoreType.DMA((5,)),
        ),
        params=pltpu.CompilerParams(vmem_limit_bytes=48 * 1024 * 1024),
        name="prepare",
    )
    pay = lax.ppermute(pay, ("dp", "expert"), swap)
    arrived = lax.all_to_all(sorted_x.reshape(dp, 32, WID), "dp", split_axis=0, concat_axis=0, tiled=True)
    moved_x = lax.ppermute(arrived.reshape(TOK, WID), ("dp", "expert"), swap)

    blocks = call(
        split_kernel,
        [struct((512, 1024))] * 4,
        (me_arr, w_up[0], w_down[0], arrived),
        in_specs=[SM, HBM, HBM, pl.BlockSpec(memory_space=pl.ANY)],
        out_spec=HBM,
        scratch=(pltpu.SemaphoreType.DMA((8,)),),
        name="split",
    )
    pay, moved_x, blocks = lax.optimization_barrier((pay, moved_x, blocks))
    blocks = [
        lax.ppermute(block, "dp", [(i, (i + k) % dp) for i in range(dp)]) if k else block
        for k, block in enumerate(blocks)
    ]
    send = call(
        pack_kernel,
        struct((128, 48, LANE)),
        (pay, moved_x),
        scratch=(pltpu.VMEM((CAP, TOK, LANE), F32), pltpu.VMEM((TOK, 2 * WID), BF)),
        name="pack",
    )
    got = lax.cond(
        me >= 0,
        lambda v: lax.all_to_all(v, plane, split_axis=0, concat_axis=0, tiled=True),
        lambda v: v,
        send,
    )
    got, blocks = lax.optimization_barrier((got, blocks))
    weights = call(
        gather_kernel,
        struct((2, 4, 256, 1024)),
        (me_arr, *blocks),
        in_specs=[SM] + [VM] * 4,
        name="gather",
        cost=pl.CostEstimate(flops=0, bytes_accessed=GATHER_BYTES, transcendentals=0),
    )
    part = call(
        forward_kernel,
        struct((4, 4, 96, WID)),
        (me_arr, got.reshape(node, group, 48, LANE), weights),
        in_specs=[SM, VM, VM],
        scratch=(pltpu.VMEM((384, 1024), BF), pltpu.VMEM((384, 1024), BF)),
        name="forward",
    )
    part = lax.all_to_all(part, "dp", split_axis=0, concat_axis=0, tiled=True)
    grad = call(act_kernel, struct((96, 1024 + LANE)), (part,), name="act")
    grads = lax.all_gather(grad, "dp", axis=0, tiled=False)
    reply = call(
        backward_kernel,
        struct((node, group, 32, LANE)),
        (me_arr, grads, weights),
        in_specs=[SM, VM, VM],
        scratch=(pltpu.VMEM((384, 1024), BF),),
        name="backward",
    )
    back = lax.all_to_all(reply.reshape(128, 32, LANE), plane, split_axis=0, concat_axis=0, tiled=True)
    result = call(
        combine_kernel,
        struct((TOK + INFO, WID)),
        (back, pay),
        scratch=(pltpu.VMEM((128 * CAP, WID), BF), pltpu.VMEM((LANE, LANE), F32)),
        name="combine",
    )
    result = lax.ppermute(result, ("dp", "expert"), swap_back)
    return result[:TOK], result[TOK:TOK + 4, :LANE].T


def solution(mesh):
    in_specs = (
        P(("dp", "node"), "expert"),
        P(("dp", "node")),
        P(("dp", "node"), None),
        P(("dp", "node"), None),
        P(("dp", "node"), "expert"),
        P(("node", "expert"), "dp", None),
        P(("node", "expert"), "dp", None),
    )
    out_specs = (P(("dp", "node"), "expert"), P(("dp", "node"), None))
    return jax.shard_map(shards, mesh=mesh, in_specs=in_specs, out_specs=out_specs, check_vma=False)
```

```python
import functools

import jax
import jax.numpy as jnp
from jax import lax
from jax.experimental import pallas as pl
from jax.experimental.pallas import tpu as pltpu
from jax.sharding import PartitionSpec as P

BF = jnp.bfloat16
F32 = jnp.float32
CAP = 6
TOK = 128
WID = 512
LANE = 128
PARAMS = pltpu.CompilerParams(vmem_limit_bytes=20 * 1024 * 1024)
HBM_PARAMS = pltpu.CompilerParams(vmem_limit_bytes=60 * 1024 * 1024)


def iota(shape, dim):
    return lax.broadcasted_iota(jnp.int32, shape, dim)


def split(index, base):
    high = jnp.floor((index + 0.5) * (1.0 / base))
    return high, index - high * base


def order_matrix(rows, columns, source):
    row = iota((rows, 1), 0).astype(F32)
    return jnp.where(iota((rows, columns), 1).astype(F32) == source(row), 1.0, 0.0).astype(BF)


def pack_source(row):
    expert, rest = split(row, 48)
    chunk, slot = split(rest, CAP)
    return chunk * 48 + slot * 8 + expert


def unpack_source(row):
    chunk, rest = split(row, 48)
    node, slot = split(rest, CAP)
    return node * 48 + chunk * CAP + slot


def collect_source(row):
    chunk, rest = split(row, 48)
    expert, slot = split(rest, CAP)
    return jnp.where(row < 192, expert * 32 + chunk * CAP + slot, jnp.where(row < 200, (row - 192) * 32 + 24, -1.0))


def reply_matrix():
    column = iota((1, 256), 1).astype(F32)
    chunk, rest = split(column, 48)
    node, slot = split(rest, CAP)
    target = jnp.where(column < 192, node * 32 + chunk * CAP + slot, jnp.where(column < 240, node * 32 + 24, -1.0))
    return jnp.where(iota((256, 256), 0).astype(F32) == target, 1.0, 0.0).astype(BF)


def dot(a, b):
    return jnp.dot(a, b, preferred_element_type=F32)


def dot_nt(a, b):
    return lax.dot_general(a, b, (((1,), (1,)), ((), ())), preferred_element_type=F32)


def dot_tn(a, b):
    return lax.dot_general(a, b, (((0,), (0,)), ((), ())), preferred_element_type=F32)


def named_rows(info):
    experts = iota((LANE, TOK), 0).astype(F32)
    named = jnp.zeros((LANE, TOK), F32)
    for j in range(4):
        named = named + jnp.where(info[j:j + 1, :] == experts, 1.0, 0.0)
    earlier = jnp.where(iota((TOK, TOK), 0) < iota((TOK, TOK), 1), 1.0, 0.0).astype(BF)
    return named, dot(named.astype(BF), earlier)


def load(pairs, sems):
    copies = [pltpu.make_async_copy(source, target, sems.at[i]) for i, (source, target) in enumerate(pairs)]
    for copy in copies:
        copy.start()
    for copy in copies:
        copy.wait()


def feature_part(me_ref, w_ref, k):
    start = pl.multiple_of(lax.rem(me_ref[0] + k, 4) * 1024, 1024)
    return w_ref.at[:, pl.ds(start, 1024)]


def prepare_kernel(shard_step, me_ref, x_hbm, dest_hbm, down_hbm, out_ref, far_ref, x_ref, dest_ref, sems):
    load(((dest_hbm, dest_ref), (x_hbm, x_ref), (feature_part(me_ref, down_hbm, 2), far_ref)), sems)
    dest = dest_ref[...]
    target = (dest // shard_step) * 32 + (dest % TOK) // 4
    pick = jnp.where(iota((TOK, TOK), 0) == target, 1.0, 0.0).astype(BF)
    out_ref[...] = dot(pick, x_ref[...]).astype(BF).reshape(4, 32, WID)


def split_kernel(me_ref, up_hbm, down_hbm, after_ref, right_ref, left_ref, own_ref, sems):
    load((
        (up_hbm, right_ref.at[:, :4096]), (up_hbm, left_ref.at[:, :4096]),
        (feature_part(me_ref, down_hbm, 1), right_ref.at[:, 4096:]),
        (feature_part(me_ref, down_hbm, 3), left_ref.at[:, 4096:]),
        (feature_part(me_ref, down_hbm, 0), own_ref),
    ), sems)


def pack_kernel(ids_ref, dy_ref, x_ref, out_ref, slots, rows):
    named, rank = named_rows(ids_ref[...].astype(F32))
    for s in range(CAP):
        slots[s] = jnp.where(rank == float(s), named, 0.0)
    token = iota((TOK, TOK), 0)
    order = jnp.where(iota((TOK, TOK), 1) == (token % 4) * 32 + token // 4, 1.0, 0.0).astype(BF)
    rows[:, :WID] = dy_ref[...]
    rows[:, WID:] = dot(order, x_ref[...].reshape(TOK, WID)).astype(BF)
    perm = order_matrix(384, 384, pack_source)
    for pair in range(8):
        halves = []
        for block in (2 * pair, 2 * pair + 1):
            pick = jnp.concatenate([slots[s, block * 8:block * 8 + 8, :] for s in range(CAP)], axis=0).astype(BF)
            got = dot(pick, rows[...]).astype(BF)
            halves.append(jnp.concatenate([got[:, a * LANE:(a + 1) * LANE] for a in range(8)], axis=0))
        sent = dot(perm, jnp.concatenate(halves, axis=1)).astype(BF)
        for h in range(2):
            out_ref[(2 * pair + h) * 8:(2 * pair + h) * 8 + 8] = sent[:, h * LANE:(h + 1) * LANE].reshape(8, 48, LANE)


def unpack_kernel(got_ref, dy_ref, x_ref):
    perm = order_matrix(384, 384, unpack_source)
    for pair in range(4):
        for half in range(2):
            both = jnp.concatenate(
                [got_ref[half * 8:half * 8 + 8, 2 * pair + b].reshape(384, LANE) for b in range(2)], axis=1
            )
            moved = dot(perm, both).astype(BF)
            rows = slice(half * 48, half * 48 + 48)
            for a in range(8):
                for b in range(2):
                    col = b * WID + (a % 4) * LANE
                    value = moved[a * 48:a * 48 + 48, b * LANE:(b + 1) * LANE]
                    if a < 4:
                        dy_ref[pair, rows, col:col + LANE] = value
                    else:
                        x_ref[rows, pair * 1024 + col:pair * 1024 + col + LANE] = value


def hidden_kernel(me_ref, dy_ref, own, left, far, right, out_ref):
    rows = dy_ref[...].reshape(384, 1024)
    for k, w in enumerate((own, left.at[:, 4096:], far, right.at[:, 4096:])):
        block = lax.rem(me_ref[0] - k + 4, 4)
        out_ref[:, block] = dot_nt(rows, w[...]).astype(BF).reshape(4, 96, 256)


def backward_kernel(me_ref, part_ref, x_ref, own, left, right, far_low, far_high, out_ref):
    me = me_ref[0]
    perm = reply_matrix()
    score = jnp.zeros((96, 1), F32)
    pieces = []
    for shift, weights in ((0, (own,)), (3, (left,)), (1, (right,)), (2, (far_low, far_high))):
        block = lax.rem(me + shift, 4)
        grad = part_ref[0, block].astype(F32)
        for s in range(1, 4):
            grad = grad + part_ref[s, block].astype(F32)
        pre = jnp.concatenate([dot_nt(x_ref[...], w[:, :4096]) for w in weights], axis=1)
        sig = jax.nn.sigmoid(pre)
        score = score + jnp.sum(pre * sig * grad, axis=1, keepdims=True)
        grad_pre = (grad * sig * (1.0 + pre * (1.0 - sig))).astype(BF)
        width = 256 // len(weights)
        pieces += [(grad_pre[:, i * width:(i + 1) * width], w) for i, w in enumerate(weights)]
    _, slot = split(iota((96, 1), 0).astype(F32), CAP)
    scores = jnp.where(iota((96, LANE), 1).astype(F32) == slot, score, 0.0).astype(BF)
    blank = jnp.zeros((16, LANE), BF)
    for pair in range(4):
        total = sum(dot(grad_pre, w[:, pair * 1024:pair * 1024 + 1024]) for grad_pre, w in pieces).astype(BF)
        for half in range(2):
            rows = slice(half * 48, half * 48 + 48)
            stacks = []
            for b in range(2):
                parts = [total[rows, b * WID + c * LANE:b * WID + (c + 1) * LANE] for c in range(4)]
                stacks.append(jnp.concatenate(parts + [scores[rows], blank], axis=0))
            sent = dot(perm, jnp.concatenate(stacks, axis=1)).astype(BF)
            for b in range(2):
                out_ref[half * 8:half * 8 + 8, 2 * pair + b] = sent[:, b * LANE:(b + 1) * LANE].reshape(8, 32, LANE)


def combine_kernel(got_ref, ids_ref, w_ref, out_ref, score_ref, rows, scores):
    weights = w_ref[...]
    high = weights.astype(BF).astype(F32)
    middle = (weights - high).astype(BF).astype(F32)
    low = weights - high - middle
    ids = ids_ref[...].astype(F32)
    info_rows = jnp.concatenate([ids, high, middle, low], axis=0).astype(BF)
    named, rank_rows = named_rows(ids)
    eye = jnp.where(iota((TOK, TOK), 0) == iota((TOK, TOK), 1), 1.0, 0.0).astype(BF)
    rank = dot_tn(rank_rows.astype(BF), eye)
    info = dot_tn(info_rows, eye[:16])
    perm = order_matrix(208, 256, collect_source)
    for pair in range(8):
        both = jnp.concatenate(
            [got_ref[(2 * pair + h) * 8:(2 * pair + h) * 8 + 8].reshape(256, LANE) for h in range(2)], axis=1
        )
        moved = dot(perm, both)
        for h in range(2):
            block = 2 * pair + h
            half = moved[:, h * LANE:(h + 1) * LANE]
            scores[block * 8:block * 8 + 8] = half[192:200]
            for c in range(4):
                rows[block * 48:block * 48 + 48, c * LANE:(c + 1) * LANE] = half[c * 48:c * 48 + 48].astype(BF)
    lanes = iota((TOK, LANE), 1).astype(F32)
    wide = iota((TOK, 128 * CAP), 1).astype(F32)
    coefs = [jnp.zeros((TOK, 128 * CAP), F32) for _ in range(3)]
    table = scores[...].astype(BF)
    back = jnp.zeros((TOK, LANE), F32)
    for j in range(4):
        expert = info[:, j:j + 1]
        mine = expert == lanes
        slot = jnp.sum(jnp.where(mine, rank, 0.0), axis=1, keepdims=True)
        here = wide == expert * float(CAP) + slot
        for p in range(3):
            coefs[p] = jnp.where(here, info[:, 4 + 4 * p + j:5 + 4 * p + j], coefs[p])
        line = dot(jnp.where(mine, 1.0, 0.0).astype(BF), table)
        value = jnp.sum(jnp.where(lanes == slot, line, 0.0), axis=1, keepdims=True)
        back = jnp.where(lanes == float(j), value, back)
    values = rows[...]
    total = dot(coefs[0].astype(BF), values) + (dot(coefs[1].astype(BF), values) + dot(coefs[2].astype(BF), values))
    out_ref[...] = total.astype(BF)
    score_ref[...] = dot_tn(back.astype(BF), eye)[:4].astype(BF)


VM = pl.BlockSpec(memory_space=pltpu.VMEM)
SM = pl.BlockSpec(memory_space=pltpu.SMEM)
HBM = pl.BlockSpec(memory_space=pltpu.HBM)


def call(kernel, out_shape, args, in_specs=None, scratch=(), name=None, out_spec=VM, params=PARAMS):
    return pl.pallas_call(
        kernel,
        out_shape=out_shape,
        in_specs=in_specs or [VM] * len(args),
        out_specs=jax.tree.map(lambda _: out_spec, out_shape),
        scratch_shapes=list(scratch),
        compiler_params=params,
        name=name,
    )(*args)


def struct(shape):
    return jax.ShapeDtypeStruct(shape, BF)


def shards(x_rollout, dest, route_ids, route_weights, cotangent, w_up, w_down):
    dp = lax.axis_size("dp")
    node = lax.axis_size("node")
    group = lax.axis_size("expert")
    me = lax.axis_index("dp")
    me_arr = me.reshape(1).astype(jnp.int32)
    plane = ("node", "expert")
    ids = route_ids.T

    up = w_up[0]
    to_right, to_left, to_far = ([(i, (i + k) % dp) for i in range(dp)] for k in (1, dp - 1, 2))
    down = w_down[0]
    sorted_x, sent_far = call(
        functools.partial(prepare_kernel, node * TOK),
        (struct((4, 32, WID)), struct((256, 1024))),
        (me_arr, x_rollout, dest.reshape(1, TOK), down),
        in_specs=[SM] + [HBM] * 3,
        scratch=(pltpu.VMEM((TOK, WID), BF), pltpu.VMEM((1, TOK), jnp.int32), pltpu.SemaphoreType.DMA((3,))),
        params=HBM_PARAMS,
        name="prepare",
    )
    far = lax.ppermute(sent_far, "dp", to_far)
    arrived = lax.all_to_all(sorted_x, "dp", split_axis=0, concat_axis=0, tiled=True)
    sent = call(
        split_kernel,
        [struct((256, 5120)), struct((256, 5120)), struct((256, 1024))],
        (me_arr, up, down, sorted_x),
        in_specs=[SM, HBM, HBM, pl.BlockSpec(memory_space=pl.ANY)],
        scratch=(pltpu.SemaphoreType.DMA((5,)),),
        params=HBM_PARAMS,
        name="split",
    )
    arrived, sent = lax.optimization_barrier((arrived, sent))
    left = lax.ppermute(sent[0], "dp", to_right)
    right = lax.ppermute(sent[1], "dp", to_left)

    def exchange(ids, dy, x):
        send = call(
            pack_kernel,
            struct((128, 48, LANE)),
            (ids, dy, x),
            scratch=(pltpu.VMEM((CAP, TOK, LANE), F32), pltpu.VMEM((TOK, 2 * WID), BF)),
            name="pack",
        )
        return lax.all_to_all(send, plane, split_axis=0, concat_axis=0, tiled=True)

    got = lax.cond(me >= 0, exchange, lambda ids, dy, x: jnp.zeros((128, 48, LANE), BF), ids, cotangent, arrived)
    got, left, right, far = lax.optimization_barrier((got, left, right, far))
    far_low = lax.ppermute(left[:128, :4096], "dp", to_right)
    far_high = lax.ppermute(right[128:, :4096], "dp", to_left)
    rows_dy, rows_x = call(
        unpack_kernel,
        (struct((4, 96, 1024)), struct((96, 4096))),
        (got.reshape(node, group, 48, LANE),),
        name="unpack",
    )
    rows_dy = lax.all_to_all(rows_dy, "dp", split_axis=0, concat_axis=0, tiled=True)
    part = call(
        hidden_kernel,
        struct((4, 4, 96, 256)),
        (me_arr, rows_dy, sent[2], left, far, right),
        in_specs=[SM] + [VM] * 5,
        name="hidden",
    )
    part = lax.all_to_all(part, "dp", split_axis=0, concat_axis=0, tiled=True)
    reply = call(
        backward_kernel,
        struct((node, group, 32, LANE)),
        (me_arr, part, rows_x, up, left, right, far_low, far_high),
        in_specs=[SM] + [VM] * 7,
        name="backward",
    )
    back = lax.all_to_all(reply.reshape(128, 32, LANE), plane, split_axis=0, concat_axis=0, tiled=True)
    grads, scores = call(
        combine_kernel,
        (struct((TOK, WID)), struct((4, TOK))),
        (back, ids, route_weights.T),
        scratch=(pltpu.VMEM((128 * CAP, WID), BF), pltpu.VMEM((LANE, LANE), F32)),
        name="combine",
    )
    return grads, scores.T


def solution(mesh):
    in_specs = (
        P(("dp", "node"), "expert"),
        P(("dp", "node")),
        P(("dp", "node"), None),
        P(("dp", "node"), None),
        P(("dp", "node"), "expert"),
        P(("node", "expert"), "dp", None),
        P(("node", "expert"), "dp", None),
    )
    out_specs = (P(("dp", "node"), "expert"), P(("dp", "node"), None))
    return jax.shard_map(shards, mesh=mesh, in_specs=in_specs, out_specs=out_specs, check_vma=False)
```

```python
import functools

import jax
import jax.numpy as jnp
from jax import lax
from jax.experimental import pallas as pl
from jax.experimental.pallas import tpu as pltpu
from jax.sharding import PartitionSpec as P

BF = jnp.bfloat16
F32 = jnp.float32
CAP = 6
TOK = 128
WID = 512
LANE = 128
PARAMS = pltpu.CompilerParams(vmem_limit_bytes=20 * 1024 * 1024)
HBM_PARAMS = pltpu.CompilerParams(vmem_limit_bytes=60 * 1024 * 1024)


def iota(shape, dim):
    return lax.broadcasted_iota(jnp.int32, shape, dim)


def split(index, base):
    high = jnp.floor((index + 0.5) * (1.0 / base))
    return high, index - high * base


def order_matrix(rows, columns, source):
    row = iota((rows, 1), 0).astype(F32)
    return jnp.where(iota((rows, columns), 1).astype(F32) == source(row), 1.0, 0.0).astype(BF)


def pack_source(row):
    expert, rest = split(row, 48)
    chunk, slot = split(rest, CAP)
    return chunk * 48 + slot * 8 + expert


def unpack_source(row):
    chunk, rest = split(row, 48)
    node, slot = split(rest, CAP)
    return node * 48 + chunk * CAP + slot


def collect_source(row):
    chunk, rest = split(row, 48)
    expert, slot = split(rest, CAP)
    return jnp.where(row < 192, expert * 32 + chunk * CAP + slot, jnp.where(row < 200, (row - 192) * 32 + 24, -1.0))


def reply_matrix():
    column = iota((1, 256), 1).astype(F32)
    chunk, rest = split(column, 48)
    node, slot = split(rest, CAP)
    target = jnp.where(column < 192, node * 32 + chunk * CAP + slot, jnp.where(column < 240, node * 32 + 24, -1.0))
    return jnp.where(iota((256, 256), 0).astype(F32) == target, 1.0, 0.0).astype(BF)


def dot(a, b):
    return jnp.dot(a, b, preferred_element_type=F32)


def dot_nt(a, b):
    return lax.dot_general(a, b, (((1,), (1,)), ((), ())), preferred_element_type=F32)


def dot_tn(a, b):
    return lax.dot_general(a, b, (((0,), (0,)), ((), ())), preferred_element_type=F32)


def named_rows(info):
    experts = iota((LANE, TOK), 0).astype(F32)
    named = jnp.zeros((LANE, TOK), F32)
    for j in range(4):
        named = named + jnp.where(info[j:j + 1, :] == experts, 1.0, 0.0)
    earlier = jnp.where(iota((TOK, TOK), 0) < iota((TOK, TOK), 1), 1.0, 0.0).astype(BF)
    return named, dot(named.astype(BF), earlier)


def load(pairs, sems):
    copies = [pltpu.make_async_copy(source, target, sems.at[i]) for i, (source, target) in enumerate(pairs)]
    for copy in copies:
        copy.start()
    for copy in copies:
        copy.wait()


def feature_part(me_ref, w_ref, k):
    start = pl.multiple_of(lax.rem(me_ref[0] + k, 4) * 1024, 1024)
    return w_ref.at[:, pl.ds(start, 1024)]


def prepare_kernel(shard_step, me_ref, x_hbm, dest_hbm, down_hbm, out_ref, far_ref, x_ref, dest_ref, sems):
    load(((dest_hbm, dest_ref), (x_hbm, x_ref), (feature_part(me_ref, down_hbm, 2), far_ref)), sems)
    dest = dest_ref[...]
    target = (dest // shard_step) * 32 + (dest % TOK) // 4
    pick = jnp.where(iota((TOK, TOK), 0) == target, 1.0, 0.0).astype(BF)
    out_ref[...] = dot(pick, x_ref[...]).astype(BF).reshape(4, 32, WID)


def split_kernel(me_ref, up_hbm, down_hbm, after_ref, right_ref, left_ref, own_ref, sems):
    load((
        (up_hbm, right_ref.at[:, :4096]), (up_hbm, left_ref.at[:, :4096]),
        (feature_part(me_ref, down_hbm, 1), right_ref.at[:, 4096:]),
        (feature_part(me_ref, down_hbm, 3), left_ref.at[:, 4096:]),
        (feature_part(me_ref, down_hbm, 0), own_ref),
    ), sems)


def pack_kernel(ids_ref, dy_ref, x_ref, out_ref, slots, rows):
    named, rank = named_rows(ids_ref[...].astype(F32))
    for s in range(CAP):
        slots[s] = jnp.where(rank == float(s), named, 0.0)
    token = iota((TOK, TOK), 0)
    order = jnp.where(iota((TOK, TOK), 1) == (token % 4) * 32 + token // 4, 1.0, 0.0).astype(BF)
    rows[:, :WID] = dy_ref[...]
    rows[:, WID:] = dot(order, x_ref[...].reshape(TOK, WID)).astype(BF)
    perm = order_matrix(384, 384, pack_source)
    for pair in range(8):
        halves = []
        for block in (2 * pair, 2 * pair + 1):
            pick = jnp.concatenate([slots[s, block * 8:block * 8 + 8, :] for s in range(CAP)], axis=0).astype(BF)
            got = dot(pick, rows[...]).astype(BF)
            halves.append(jnp.concatenate([got[:, a * LANE:(a + 1) * LANE] for a in range(8)], axis=0))
        sent = dot(perm, jnp.concatenate(halves, axis=1)).astype(BF)
        for h in range(2):
            out_ref[(2 * pair + h) * 8:(2 * pair + h) * 8 + 8] = sent[:, h * LANE:(h + 1) * LANE].reshape(8, 48, LANE)


def unpack_kernel(got_ref, dy_ref, x_ref):
    perm = order_matrix(384, 384, unpack_source)
    for pair in range(4):
        for half in range(2):
            both = jnp.concatenate(
                [got_ref[half * 8:half * 8 + 8, 2 * pair + b].reshape(384, LANE) for b in range(2)], axis=1
            )
            moved = dot(perm, both).astype(BF)
            rows = slice(half * 48, half * 48 + 48)
            for a in range(8):
                for b in range(2):
                    col = b * WID + (a % 4) * LANE
                    value = moved[a * 48:a * 48 + 48, b * LANE:(b + 1) * LANE]
                    if a < 4:
                        dy_ref[pair, rows, col:col + LANE] = value
                    else:
                        x_ref[rows, pair * 1024 + col:pair * 1024 + col + LANE] = value


def hidden_kernel(me_ref, dy_ref, own, left, far, right, out_ref):
    rows = dy_ref[...].reshape(384, 1024)
    for k, w in enumerate((own, left.at[:, 4096:], far, right.at[:, 4096:])):
        block = lax.rem(me_ref[0] - k + 4, 4)
        out_ref[:, block] = dot_nt(rows, w[...]).astype(BF).reshape(4, 96, 256)


def backward_kernel(me_ref, part_ref, x_ref, own, left, right, far_low, far_high, out_ref):
    me = me_ref[0]
    perm = reply_matrix()
    score = jnp.zeros((96, 1), F32)
    pieces = []
    for shift, weights in ((0, (own,)), (3, (left,)), (1, (right,)), (2, (far_low, far_high))):
        block = lax.rem(me + shift, 4)
        grad = part_ref[0, block].astype(F32)
        for s in range(1, 4):
            grad = grad + part_ref[s, block].astype(F32)
        pre = jnp.concatenate([dot_nt(x_ref[...], w[:, :4096]) for w in weights], axis=1)
        sig = jax.nn.sigmoid(pre)
        score = score + jnp.sum(pre * sig * grad, axis=1, keepdims=True)
        grad_pre = (grad * sig * (1.0 + pre * (1.0 - sig))).astype(BF)
        width = 256 // len(weights)
        pieces += [(grad_pre[:, i * width:(i + 1) * width], w) for i, w in enumerate(weights)]
    _, slot = split(iota((96, 1), 0).astype(F32), CAP)
    scores = jnp.where(iota((96, LANE), 1).astype(F32) == slot, score, 0.0).astype(BF)
    blank = jnp.zeros((16, LANE), BF)
    for pair in range(4):
        total = sum(dot(grad_pre, w[:, pair * 1024:pair * 1024 + 1024]) for grad_pre, w in pieces).astype(BF)
        for half in range(2):
            rows = slice(half * 48, half * 48 + 48)
            stacks = []
            for b in range(2):
                parts = [total[rows, b * WID + c * LANE:b * WID + (c + 1) * LANE] for c in range(4)]
                stacks.append(jnp.concatenate(parts + [scores[rows], blank], axis=0))
            sent = dot(perm, jnp.concatenate(stacks, axis=1)).astype(BF)
            for b in range(2):
                out_ref[half * 8:half * 8 + 8, 2 * pair + b] = sent[:, b * LANE:(b + 1) * LANE].reshape(8, 32, LANE)


def combine_kernel(got_ref, ids_ref, w_ref, out_ref, score_ref, rows, scores):
    weights = w_ref[...]
    high = weights.astype(BF).astype(F32)
    middle = (weights - high).astype(BF).astype(F32)
    low = weights - high - middle
    ids = ids_ref[...].astype(F32)
    info_rows = jnp.concatenate([ids, high, middle, low], axis=0).astype(BF)
    named, rank_rows = named_rows(ids)
    eye = jnp.where(iota((TOK, TOK), 0) == iota((TOK, TOK), 1), 1.0, 0.0).astype(BF)
    rank = dot_tn(rank_rows.astype(BF), eye)
    info = dot_tn(info_rows, eye[:16])
    perm = order_matrix(208, 256, collect_source)
    for pair in range(8):
        both = jnp.concatenate(
            [got_ref[(2 * pair + h) * 8:(2 * pair + h) * 8 + 8].reshape(256, LANE) for h in range(2)], axis=1
        )
        moved = dot(perm, both)
        for h in range(2):
            block = 2 * pair + h
            half = moved[:, h * LANE:(h + 1) * LANE]
            scores[block * 8:block * 8 + 8] = half[192:200]
            for c in range(4):
                rows[block * 48:block * 48 + 48, c * LANE:(c + 1) * LANE] = half[c * 48:c * 48 + 48].astype(BF)
    lanes = iota((TOK, LANE), 1).astype(F32)
    wide = iota((TOK, 128 * CAP), 1).astype(F32)
    coefs = [jnp.zeros((TOK, 128 * CAP), F32) for _ in range(3)]
    table = scores[...].astype(BF)
    back = jnp.zeros((TOK, LANE), F32)
    for j in range(4):
        expert = info[:, j:j + 1]
        mine = expert == lanes
        slot = jnp.sum(jnp.where(mine, rank, 0.0), axis=1, keepdims=True)
        here = wide == expert * float(CAP) + slot
        for p in range(3):
            coefs[p] = jnp.where(here, info[:, 4 + 4 * p + j:5 + 4 * p + j], coefs[p])
        line = dot(jnp.where(mine, 1.0, 0.0).astype(BF), table)
        value = jnp.sum(jnp.where(lanes == slot, line, 0.0), axis=1, keepdims=True)
        back = jnp.where(lanes == float(j), value, back)
    values = rows[...]
    total = dot(coefs[0].astype(BF), values) + (dot(coefs[1].astype(BF), values) + dot(coefs[2].astype(BF), values))
    out_ref[...] = total.astype(BF)
    score_ref[...] = dot_tn(back.astype(BF), eye)[:4].astype(BF)


VM = pl.BlockSpec(memory_space=pltpu.VMEM)
SM = pl.BlockSpec(memory_space=pltpu.SMEM)
HBM = pl.BlockSpec(memory_space=pltpu.HBM)


def call(kernel, out_shape, args, in_specs=None, scratch=(), name=None, out_spec=VM, params=PARAMS):
    return pl.pallas_call(
        kernel,
        out_shape=out_shape,
        in_specs=in_specs or [VM] * len(args),
        out_specs=jax.tree.map(lambda _: out_spec, out_shape),
        scratch_shapes=list(scratch),
        compiler_params=params,
        name=name,
    )(*args)


def struct(shape):
    return jax.ShapeDtypeStruct(shape, BF)


def shards(x_rollout, dest, route_ids, route_weights, cotangent, w_up, w_down):
    dp = lax.axis_size("dp")
    node = lax.axis_size("node")
    group = lax.axis_size("expert")
    me = lax.axis_index("dp")
    me_arr = me.reshape(1).astype(jnp.int32)
    plane = ("node", "expert")
    ids = route_ids.T

    up = w_up[0]
    to_right, to_left, to_far = ([(i, (i + k) % dp) for i in range(dp)] for k in (1, dp - 1, 2))
    down = w_down[0]
    sorted_x, sent_far = call(
        functools.partial(prepare_kernel, node * TOK),
        (struct((4, 32, WID)), struct((256, 1024))),
        (me_arr, x_rollout, dest.reshape(1, TOK), down),
        in_specs=[SM] + [HBM] * 3,
        scratch=(pltpu.VMEM((TOK, WID), BF), pltpu.VMEM((1, TOK), jnp.int32), pltpu.SemaphoreType.DMA((3,))),
        params=HBM_PARAMS,
        name="prepare",
    )
    far = lax.ppermute(sent_far, "dp", to_far)
    arrived = lax.all_to_all(sorted_x, "dp", split_axis=0, concat_axis=0, tiled=True)
    sent = call(
        split_kernel,
        [struct((256, 5120)), struct((256, 5120)), struct((256, 1024))],
        (me_arr, up, down, sorted_x),
        in_specs=[SM, HBM, HBM, pl.BlockSpec(memory_space=pl.ANY)],
        scratch=(pltpu.SemaphoreType.DMA((5,)),),
        params=HBM_PARAMS,
        name="split",
    )
    arrived, sent = lax.optimization_barrier((arrived, sent))
    left = lax.ppermute(sent[0], "dp", to_right)
    right = lax.ppermute(sent[1], "dp", to_left)

    def exchange(ids, dy, x):
        send = call(
            pack_kernel,
            struct((128, 48, LANE)),
            (ids, dy, x),
            scratch=(pltpu.VMEM((CAP, TOK, LANE), F32), pltpu.VMEM((TOK, 2 * WID), BF)),
            name="pack",
        )
        got = lax.all_to_all(send, plane, split_axis=0, concat_axis=0, tiled=True)
        return call(
            unpack_kernel,
            (struct((4, 96, 1024)), struct((96, 4096))),
            (got.reshape(node, group, 48, LANE),),
            name="unpack",
        )

    def nothing(ids, dy, x):
        return jnp.zeros((4, 96, 1024), BF), jnp.zeros((96, 4096), BF)

    rows_dy, rows_x = lax.cond(me >= 0, exchange, nothing, ids, cotangent, arrived)
    rows_dy, rows_x, left, right, far = lax.optimization_barrier((rows_dy, rows_x, left, right, far))
    far_low = lax.ppermute(left[:128, :4096], "dp", to_right)
    far_high = lax.ppermute(right[128:, :4096], "dp", to_left)
    rows_dy = lax.all_to_all(rows_dy, "dp", split_axis=0, concat_axis=0, tiled=True)
    part = call(
        hidden_kernel,
        struct((4, 4, 96, 256)),
        (me_arr, rows_dy, sent[2], left, far, right),
        in_specs=[SM] + [VM] * 5,
        name="hidden",
    )
    part = lax.all_to_all(part, "dp", split_axis=0, concat_axis=0, tiled=True)
    reply = call(
        backward_kernel,
        struct((node, group, 32, LANE)),
        (me_arr, part, rows_x, up, left, right, far_low, far_high),
        in_specs=[SM] + [VM] * 7,
        name="backward",
    )
    back = lax.all_to_all(reply.reshape(128, 32, LANE), plane, split_axis=0, concat_axis=0, tiled=True)
    grads, scores = call(
        combine_kernel,
        (struct((TOK, WID)), struct((4, TOK))),
        (back, ids, route_weights.T),
        scratch=(pltpu.VMEM((128 * CAP, WID), BF), pltpu.VMEM((LANE, LANE), F32)),
        name="combine",
    )
    return grads, scores.T


def solution(mesh):
    in_specs = (
        P(("dp", "node"), "expert"),
        P(("dp", "node")),
        P(("dp", "node"), None),
        P(("dp", "node"), None),
        P(("dp", "node"), "expert"),
        P(("node", "expert"), "dp", None),
        P(("node", "expert"), "dp", None),
    )
    out_specs = (P(("dp", "node"), "expert"), P(("dp", "node"), None))
    return jax.shard_map(shards, mesh=mesh, in_specs=in_specs, out_specs=out_specs, check_vma=False)
```

```python
import functools

import jax
import jax.numpy as jnp
from jax import lax
from jax.experimental import pallas as pl
from jax.experimental.pallas import tpu as pltpu
from jax.sharding import PartitionSpec as P

BF = jnp.bfloat16
F32 = jnp.float32
CAP = 6
TOK = 128
WID = 512
LANE = 128
PARAMS = pltpu.CompilerParams(vmem_limit_bytes=20 * 1024 * 1024)
HBM_PARAMS = pltpu.CompilerParams(vmem_limit_bytes=60 * 1024 * 1024)


def iota(shape, dim):
    return lax.broadcasted_iota(jnp.int32, shape, dim)


def split(index, base):
    high = jnp.floor((index + 0.5) * (1.0 / base))
    return high, index - high * base


def order_matrix(rows, columns, source):
    row = iota((rows, 1), 0).astype(F32)
    return jnp.where(iota((rows, columns), 1).astype(F32) == source(row), 1.0, 0.0).astype(BF)


def pack_source(row):
    expert, rest = split(row, 48)
    chunk, slot = split(rest, CAP)
    return chunk * 48 + slot * 8 + expert


def unpack_source(row):
    chunk, rest = split(row, 48)
    node, slot = split(rest, CAP)
    return node * 48 + chunk * CAP + slot


def collect_source(row):
    chunk, rest = split(row, 48)
    expert, slot = split(rest, CAP)
    return jnp.where(row < 192, expert * 32 + chunk * CAP + slot, jnp.where(row < 200, (row - 192) * 32 + 24, -1.0))


def reply_matrix():
    column = iota((1, 256), 1).astype(F32)
    chunk, rest = split(column, 48)
    node, slot = split(rest, CAP)
    target = jnp.where(column < 192, node * 32 + chunk * CAP + slot, jnp.where(column < 240, node * 32 + 24, -1.0))
    return jnp.where(iota((256, 256), 0).astype(F32) == target, 1.0, 0.0).astype(BF)


def dot(a, b):
    return jnp.dot(a, b, preferred_element_type=F32)


def dot_nt(a, b):
    return lax.dot_general(a, b, (((1,), (1,)), ((), ())), preferred_element_type=F32)


def dot_tn(a, b):
    return lax.dot_general(a, b, (((0,), (0,)), ((), ())), preferred_element_type=F32)


def named_rows(info):
    experts = iota((LANE, TOK), 0).astype(F32)
    named = jnp.zeros((LANE, TOK), F32)
    for j in range(4):
        named = named + jnp.where(info[j:j + 1, :] == experts, 1.0, 0.0)
    earlier = jnp.where(iota((TOK, TOK), 0) < iota((TOK, TOK), 1), 1.0, 0.0).astype(BF)
    return named, dot(named.astype(BF), earlier)


def load(pairs, sems):
    copies = [pltpu.make_async_copy(source, target, sems.at[i]) for i, (source, target) in enumerate(pairs)]
    for copy in copies:
        copy.start()
    for copy in copies:
        copy.wait()


def feature_part(me_ref, w_ref, k):
    start = pl.multiple_of(lax.rem(me_ref[0] + k, 4) * 1024, 1024)
    return w_ref.at[:, pl.ds(start, 1024)]


def prepare_kernel(shard_step, me_ref, x_hbm, dest_hbm, down_hbm, out_ref, far_ref, x_ref, dest_ref, sems):
    load(((dest_hbm, dest_ref), (x_hbm, x_ref), (feature_part(me_ref, down_hbm, 2), far_ref)), sems)
    dest = dest_ref[...]
    target = (dest // shard_step) * 32 + (dest % TOK) // 4
    pick = jnp.where(iota((TOK, TOK), 0) == target, 1.0, 0.0).astype(BF)
    out_ref[...] = dot(pick, x_ref[...]).astype(BF).reshape(4, 32, WID)


def split_kernel(me_ref, up_hbm, down_hbm, after_ref, right_ref, left_ref, own_ref, sems):
    load((
        (up_hbm, right_ref.at[:, :4096]), (up_hbm, left_ref.at[:, :4096]),
        (feature_part(me_ref, down_hbm, 1), right_ref.at[:, 4096:]),
        (feature_part(me_ref, down_hbm, 3), left_ref.at[:, 4096:]),
        (feature_part(me_ref, down_hbm, 0), own_ref),
    ), sems)


def pack_kernel(ids_ref, dy_ref, x_ref, out_ref, slots, rows):
    named, rank = named_rows(ids_ref[...].astype(F32))
    for s in range(CAP):
        slots[s] = jnp.where(rank == float(s), named, 0.0)
    token = iota((TOK, TOK), 0)
    order = jnp.where(iota((TOK, TOK), 1) == (token % 4) * 32 + token // 4, 1.0, 0.0).astype(BF)
    rows[:, :WID] = dy_ref[...]
    rows[:, WID:] = dot(order, x_ref[...].reshape(TOK, WID)).astype(BF)
    perm = order_matrix(384, 384, pack_source)
    for pair in range(8):
        halves = []
        for block in (2 * pair, 2 * pair + 1):
            pick = jnp.concatenate([slots[s, block * 8:block * 8 + 8, :] for s in range(CAP)], axis=0).astype(BF)
            got = dot(pick, rows[...]).astype(BF)
            halves.append(jnp.concatenate([got[:, a * LANE:(a + 1) * LANE] for a in range(8)], axis=0))
        sent = dot(perm, jnp.concatenate(halves, axis=1)).astype(BF)
        for h in range(2):
            out_ref[(2 * pair + h) * 8:(2 * pair + h) * 8 + 8] = sent[:, h * LANE:(h + 1) * LANE].reshape(8, 48, LANE)


def unpack_kernel(got_ref, dy_ref, x_ref):
    perm = order_matrix(384, 384, unpack_source)
    for pair in range(4):
        for half in range(2):
            both = jnp.concatenate(
                [got_ref[half * 8:half * 8 + 8, 2 * pair + b].reshape(384, LANE) for b in range(2)], axis=1
            )
            moved = dot(perm, both).astype(BF)
            rows = slice(half * 48, half * 48 + 48)
            for a in range(8):
                for b in range(2):
                    col = b * WID + (a % 4) * LANE
                    value = moved[a * 48:a * 48 + 48, b * LANE:(b + 1) * LANE]
                    if a < 4:
                        dy_ref[pair, rows, col:col + LANE] = value
                    else:
                        x_ref[rows, pair * 1024 + col:pair * 1024 + col + LANE] = value


def halves_kernel(left, right, low_ref, high_ref, sems):
    load(((left.at[:128, :4096], low_ref), (right.at[128:, :4096], high_ref)), sems)


def hidden_kernel(me_ref, dy_ref, own, left, far, right, out_ref):
    rows = dy_ref[...].reshape(384, 1024)
    for k, w in enumerate((own, left.at[:, 4096:], far, right.at[:, 4096:])):
        block = lax.rem(me_ref[0] - k + 4, 4)
        out_ref[:, block] = dot_nt(rows, w[...]).astype(BF).reshape(4, 96, 256)


def backward_kernel(me_ref, part_ref, x_ref, own, left, right, far_low, far_high, out_ref):
    me = me_ref[0]
    perm = reply_matrix()
    score = jnp.zeros((96, 1), F32)
    pieces = []
    for shift, weights in ((0, (own,)), (3, (left,)), (1, (right,)), (2, (far_low, far_high))):
        block = lax.rem(me + shift, 4)
        grad = part_ref[0, block].astype(F32)
        for s in range(1, 4):
            grad = grad + part_ref[s, block].astype(F32)
        pre = jnp.concatenate([dot_nt(x_ref[...], w[:, :4096]) for w in weights], axis=1)
        sig = jax.nn.sigmoid(pre)
        score = score + jnp.sum(pre * sig * grad, axis=1, keepdims=True)
        grad_pre = (grad * sig * (1.0 + pre * (1.0 - sig))).astype(BF)
        width = 256 // len(weights)
        pieces += [(grad_pre[:, i * width:(i + 1) * width], w) for i, w in enumerate(weights)]
    _, slot = split(iota((96, 1), 0).astype(F32), CAP)
    scores = jnp.where(iota((96, LANE), 1).astype(F32) == slot, score, 0.0).astype(BF)
    blank = jnp.zeros((16, LANE), BF)
    for pair in range(4):
        total = sum(dot(grad_pre, w[:, pair * 1024:pair * 1024 + 1024]) for grad_pre, w in pieces).astype(BF)
        for half in range(2):
            rows = slice(half * 48, half * 48 + 48)
            stacks = []
            for b in range(2):
                parts = [total[rows, b * WID + c * LANE:b * WID + (c + 1) * LANE] for c in range(4)]
                stacks.append(jnp.concatenate(parts + [scores[rows], blank], axis=0))
            sent = dot(perm, jnp.concatenate(stacks, axis=1)).astype(BF)
            for b in range(2):
                out_ref[half * 8:half * 8 + 8, 2 * pair + b] = sent[:, b * LANE:(b + 1) * LANE].reshape(8, 32, LANE)


def combine_kernel(got_ref, ids_ref, w_ref, out_ref, score_ref, rows, scores):
    weights = w_ref[...]
    high = weights.astype(BF).astype(F32)
    middle = (weights - high).astype(BF).astype(F32)
    low = weights - high - middle
    ids = ids_ref[...].astype(F32)
    info_rows = jnp.concatenate([ids, high, middle, low], axis=0).astype(BF)
    named, rank_rows = named_rows(ids)
    eye = jnp.where(iota((TOK, TOK), 0) == iota((TOK, TOK), 1), 1.0, 0.0).astype(BF)
    rank = dot_tn(rank_rows.astype(BF), eye)
    info = dot_tn(info_rows, eye[:16])
    perm = order_matrix(208, 256, collect_source)
    for pair in range(8):
        both = jnp.concatenate(
            [got_ref[(2 * pair + h) * 8:(2 * pair + h) * 8 + 8].reshape(256, LANE) for h in range(2)], axis=1
        )
        moved = dot(perm, both)
        for h in range(2):
            block = 2 * pair + h
            half = moved[:, h * LANE:(h + 1) * LANE]
            scores[block * 8:block * 8 + 8] = half[192:200]
            for c in range(4):
                rows[block * 48:block * 48 + 48, c * LANE:(c + 1) * LANE] = half[c * 48:c * 48 + 48].astype(BF)
    lanes = iota((TOK, LANE), 1).astype(F32)
    wide = iota((TOK, 128 * CAP), 1).astype(F32)
    coefs = [jnp.zeros((TOK, 128 * CAP), F32) for _ in range(3)]
    table = scores[...].astype(BF)
    back = jnp.zeros((TOK, LANE), F32)
    for j in range(4):
        expert = info[:, j:j + 1]
        mine = expert == lanes
        slot = jnp.sum(jnp.where(mine, rank, 0.0), axis=1, keepdims=True)
        here = wide == expert * float(CAP) + slot
        for p in range(3):
            coefs[p] = jnp.where(here, info[:, 4 + 4 * p + j:5 + 4 * p + j], coefs[p])
        line = dot(jnp.where(mine, 1.0, 0.0).astype(BF), table)
        value = jnp.sum(jnp.where(lanes == slot, line, 0.0), axis=1, keepdims=True)
        back = jnp.where(lanes == float(j), value, back)
    values = rows[...]
    total = dot(coefs[0].astype(BF), values) + (dot(coefs[1].astype(BF), values) + dot(coefs[2].astype(BF), values))
    out_ref[...] = total.astype(BF)
    score_ref[...] = dot_tn(back.astype(BF), eye)[:4].astype(BF)


VM = pl.BlockSpec(memory_space=pltpu.VMEM)
SM = pl.BlockSpec(memory_space=pltpu.SMEM)
HBM = pl.BlockSpec(memory_space=pltpu.HBM)


def call(kernel, out_shape, args, in_specs=None, scratch=(), name=None, out_spec=VM, params=PARAMS):
    return pl.pallas_call(
        kernel,
        out_shape=out_shape,
        in_specs=in_specs or [VM] * len(args),
        out_specs=jax.tree.map(lambda _: out_spec, out_shape),
        scratch_shapes=list(scratch),
        compiler_params=params,
        name=name,
    )(*args)


def struct(shape):
    return jax.ShapeDtypeStruct(shape, BF)


def shards(x_rollout, dest, route_ids, route_weights, cotangent, w_up, w_down):
    dp = lax.axis_size("dp")
    node = lax.axis_size("node")
    group = lax.axis_size("expert")
    me = lax.axis_index("dp")
    me_arr = me.reshape(1).astype(jnp.int32)
    plane = ("node", "expert")
    ids = route_ids.T

    up = w_up[0]
    to_right, to_left, to_far = ([(i, (i + k) % dp) for i in range(dp)] for k in (1, dp - 1, 2))
    down = w_down[0]
    sorted_x, sent_far = call(
        functools.partial(prepare_kernel, node * TOK),
        (struct((4, 32, WID)), struct((256, 1024))),
        (me_arr, x_rollout, dest.reshape(1, TOK), down),
        in_specs=[SM] + [HBM] * 3,
        scratch=(pltpu.VMEM((TOK, WID), BF), pltpu.VMEM((1, TOK), jnp.int32), pltpu.SemaphoreType.DMA((3,))),
        params=HBM_PARAMS,
        name="prepare",
    )
    far = lax.ppermute(sent_far, "dp", to_far)
    arrived = lax.all_to_all(sorted_x, "dp", split_axis=0, concat_axis=0, tiled=True)
    sent = call(
        split_kernel,
        [struct((256, 5120)), struct((256, 5120)), struct((256, 1024))],
        (me_arr, up, down, sorted_x),
        in_specs=[SM, HBM, HBM, pl.BlockSpec(memory_space=pl.ANY)],
        scratch=(pltpu.SemaphoreType.DMA((5,)),),
        params=HBM_PARAMS,
        name="split",
    )
    arrived, sent = lax.optimization_barrier((arrived, sent))
    left = lax.ppermute(sent[0], "dp", to_right)
    right = lax.ppermute(sent[1], "dp", to_left)

    def exchange(ids, dy, x):
        send = call(
            pack_kernel,
            struct((128, 48, LANE)),
            (ids, dy, x),
            scratch=(pltpu.VMEM((CAP, TOK, LANE), F32), pltpu.VMEM((TOK, 2 * WID), BF)),
            name="pack",
        )
        got = lax.all_to_all(send, plane, split_axis=0, concat_axis=0, tiled=True)
        return call(
            unpack_kernel,
            (struct((4, 96, 1024)), struct((96, 4096))),
            (got.reshape(node, group, 48, LANE),),
            name="unpack",
        )

    def nothing(ids, dy, x):
        return jnp.zeros((4, 96, 1024), BF), jnp.zeros((96, 4096), BF)

    rows_dy, rows_x = lax.cond(me >= 0, exchange, nothing, ids, cotangent, arrived)
    rows_dy, rows_x, left, right, far = lax.optimization_barrier((rows_dy, rows_x, left, right, far))
    low, high = call(
        halves_kernel,
        (struct((128, 4096)), struct((128, 4096))),
        (left, right),
        in_specs=[pl.BlockSpec(memory_space=pl.ANY)] * 2,
        scratch=(pltpu.SemaphoreType.DMA((2,)),),
        name="halves",
    )
    far_low = lax.ppermute(low, "dp", to_right)
    far_high = lax.ppermute(high, "dp", to_left)
    rows_dy = lax.all_to_all(rows_dy, "dp", split_axis=0, concat_axis=0, tiled=True)
    part = call(
        hidden_kernel,
        struct((4, 4, 96, 256)),
        (me_arr, rows_dy, sent[2], left, far, right),
        in_specs=[SM] + [VM] * 5,
        name="hidden",
    )
    part = lax.all_to_all(part, "dp", split_axis=0, concat_axis=0, tiled=True)
    reply = call(
        backward_kernel,
        struct((node, group, 32, LANE)),
        (me_arr, part, rows_x, up, left, right, far_low, far_high),
        in_specs=[SM] + [VM] * 7,
        name="backward",
    )
    back = lax.all_to_all(reply.reshape(128, 32, LANE), plane, split_axis=0, concat_axis=0, tiled=True)
    grads, scores = call(
        combine_kernel,
        (struct((TOK, WID)), struct((4, TOK))),
        (back, ids, route_weights.T),
        scratch=(pltpu.VMEM((128 * CAP, WID), BF), pltpu.VMEM((LANE, LANE), F32)),
        name="combine",
    )
    return grads, scores.T


def solution(mesh):
    in_specs = (
        P(("dp", "node"), "expert"),
        P(("dp", "node")),
        P(("dp", "node"), None),
        P(("dp", "node"), None),
        P(("dp", "node"), "expert"),
        P(("node", "expert"), "dp", None),
        P(("node", "expert"), "dp", None),
    )
    out_specs = (P(("dp", "node"), "expert"), P(("dp", "node"), None))
    return jax.shard_map(shards, mesh=mesh, in_specs=in_specs, out_specs=out_specs, check_vma=False)
```
